32 devices in a mesh: group: 2 (over y), row: 4 (over z), cent: 4 (over x, core).
Axes of the slice: x: 2, y: 2, z: 4, core: 2. Of those that a mesh axis runs over, the one named last changes fastest.
Arguments:
- embeddings: bfloat16 [8, 512, 1024], P(('group', 'cent'), 'row'), parts along dimension 0, may hold values from -6 to 6
- centroids: bfloat16 [8, 2048, 1024], P(('group', 'cent'), 'row'), parts along dimension 0, may hold values from -1 to 1
- owner: int32 [8, 512, 1], P(('group', 'cent'), 'row'), parts along dimension 0, may hold values from 0 to 3; in each aligned block of 128 rows (0 to 127, 128 to 255, ..., all dimensions but the last counted through in order) at most 128 rows name the same one
- slot: int32 [8, 512], P(('group', 'cent'), 'row'), parts along dimension 0, may hold values from 0 to 511
Outputs:
- gap: float32 [8, 512], P(('group', 'cent'), 'row'), parts along dimension 0
- new_centroids: float32 [8, 2048, 1024], P(('group', 'cent'), 'row'), parts along dimension 0
The draws below stay inside these ranges and needn't reach their ends.
There are 2 independent parts, one for each index of `group`. The reference program is written for one: setup_inputs(seed, part) draws one part's arguments, and reference() takes and returns one part's arrays. A program takes and returns all parts, laid end to end along the dimension named above; each array names one. Nothing has to cross between parts.
Inputs may be any that keep to these rules, and one draw needn't show every extreme that they name: Among the 128 rows of one device, at most 128 have the same owner, and in every draw some device has exactly 128 rows with one owner.
All inputs are finite; a program needn't handle non-finite values.
Results may differ from the reference program's by a relative error of at most 0.0003.
Values may be sent and summed in bfloat16 or wider, within the bound.
A program may use at most 64 MiB of HBM per device.

```python
import math
import jax
import jax.numpy as jnp
import numpy as np
from jax import lax

D = 1024
K_DEV = 512
ROW_DEV = 128
L1 = 4
CROWS = 512
CHILD = 2048
CAP = 128
N_ROW = 4


def draw_centroids(key, part):
    key = jax.random.fold_in(key, 11)
    scale_key, value_key = jax.random.split(key)
    spread = jnp.exp(jax.random.uniform(scale_key, (L1, CHILD, 1), jnp.float32, jnp.log(0.5), jnp.log(2.0)))
    values = jnp.clip(jax.random.normal(value_key, (L1, CHILD, D), jnp.float32), -6.0, 6.0)
    return jnp.clip(spread * values * D ** (-0.5), -1.0, 1.0).astype(jnp.bfloat16)


def with_ends(entries, own_key, least, top_value):
    spot = [jax.random.randint(jax.random.fold_in(own_key, axis), (), 0, length) for axis, length in enumerate(entries.shape)]
    main_axis = entries.shape.index(max(entries.shape))
    beside = spot[:main_axis] + [(spot[main_axis] + 1) % entries.shape[main_axis]] + spot[main_axis + 1:]
    return entries.at[tuple(spot)].set(least).at[tuple(beside)].set(top_value)


def shard_levels(key, shape, pieces, least, top_value):
    factor_of, own = 1.0, jax.random.fold_in(key, 6)
    for dim, blocks in pieces:
        draws = jnp.exp(jax.random.uniform(jax.random.fold_in(own, dim), (blocks,), jnp.float32, least / len(pieces), top_value / len(pieces)))
        factor_of = factor_of * jnp.repeat(draws, shape[dim] // blocks).reshape([-1 if axis == dim else 1 for axis in range(len(shape))])
    return factor_of


def deal_out(stream_key, own, number, rows, number_of, top, most, slope):
    sequence = jax.random.permutation(stream_key, number_of)
    crowded, usual = portions_of(number_of, rows * top, most, slope, True), portions_of(number_of, rows * top, most, slope, False)
    places = jnp.arange(number_of)

    def named(tallies, turn):
        used = int((tallies > 0).sum())
        fixed = max(1, used // 4)
        passed = fixed + (places - fixed + turn * (used - fixed)) % max(1, number_of - fixed)
        return jnp.zeros((number_of,), jnp.int32).at[sequence[jnp.where(places < fixed, places, passed)]].set(jnp.asarray(tallies, jnp.int32))

    tallies = jnp.where(number % 4 == 0, named(crowded, number // 4), named(usual, number - number // 4 - 1))
    mixed = jax.random.permutation(jax.random.fold_in(own, 3), number_of)
    source_of, taker = mixed[0:number_of // 2 * 2:2], mixed[1:number_of // 2 * 2:2]
    slack = jnp.minimum(tallies[source_of] - 1, most - tallies[taker]) // 2
    slack = jnp.where((source_of == sequence[0]) | (taker == sequence[0]) | (tallies[taker] == 0), 0, jnp.maximum(slack, 0))
    passed = jax.random.randint(jax.random.fold_in(own, 4), (number_of // 2,), 0, 1 << 20) % (slack + 1)
    tallies = tallies.at[source_of].add(-passed).at[taker].add(passed)
    labels = jnp.searchsorted(jnp.cumsum(tallies), jnp.arange(rows * top), side="right").astype(jnp.int32)
    listing = labels.reshape(top, rows).T
    listing = listing[jax.random.permutation(jax.random.fold_in(own, 1), rows)]
    turn = jax.random.randint(jax.random.fold_in(own, 2), (rows, 1), 0, top)
    return jnp.take_along_axis(listing, (jnp.arange(top)[None, :] + turn) % top, axis=1)


def portions_of(amount, total, limit, lean, full):
    weights = [(1 << 20) // math.isqrt(grade ** lean) + 1 for grade in range(1, amount + 1)]
    largest = limit if full else min(limit, max(-(-total // amount), total * weights[0] // sum(weights)))
    least = 1 if total - largest >= amount - 1 else 0
    given, surplus = [largest] + [least] * (amount - 1), total - largest - least * (amount - 1)
    while surplus > 0:
        movable = [i for i in range(1, amount) if given[i] < largest] or [i for i in range(1, amount) if given[i] < limit]
        whole, remaining = sum([weights[i] for i in movable]), surplus
        for i in movable:
            addition = min(limit - given[i], max(1, remaining * weights[i] // whole), surplus)
            given[i] = given[i] + addition
            surplus = surplus - addition
    return np.array(given)


def centred(rng, extent, scale, reach, cuts=(), kind=jnp.bfloat16):
    drawn = jax.random.normal(rng, extent, jnp.float32) * scale
    if len(cuts) > 0:
        drawn = shard_levels(rng, extent, cuts, -0.22, 0.18) * drawn
    return jnp.clip(drawn, min=-reach, max=reach).astype(kind)


def setup_inputs(seed: int = 0, part: int = 0) -> dict:
    keys = jax.random.split(jax.random.key(seed), 5)
    part_splits = jax.random.split(jax.random.fold_in(keys[4], part), 5)
    embeddings = centred(part_splits[0], (L1, CROWS, D), 1.0, 6.0, ((0, 4), (1, 4)))
    centroids = draw_centroids(jax.random.fold_in(jax.random.fold_in(keys[4], part), 71), part)
    owner_keys = jax.random.split(jax.random.fold_in(part_splits[2], 1), L1 * CROWS // ROW_DEV)
    owner_turns = jax.random.permutation(jax.random.fold_in(part_splits[2], 3), L1 * CROWS // ROW_DEV)
    owner = jax.vmap(lambda own, number: deal_out(jax.random.fold_in(part_splits[2], 2), own, number, ROW_DEV, N_ROW, 1, CAP, 2))(owner_keys, owner_turns).reshape((L1, CROWS, 1))
    slot = with_ends(jax.random.randint(part_splits[3], (L1, CROWS), 0, K_DEV), jax.random.fold_in(part_splits[3], 1), 0, K_DEV - 1).astype(jnp.int32)
    return dict(embeddings=embeddings, centroids=centroids, owner=owner, slot=slot)


def score_cluster(operands):
    embed_rows, cent_rows, owner_ids, slot_ids = operands
    half_norm = 0.5 * jnp.sum(jnp.square(cent_rows.astype(jnp.float32)), axis=1)
    cent_blocks = cent_rows.reshape(N_ROW, K_DEV, D)
    half_blocks = half_norm.reshape(N_ROW, K_DEV)
    column_ids = lax.broadcasted_iota(jnp.int32, (CROWS, K_DEV), 1)
    owner_range = jnp.arange(N_ROW, dtype=jnp.int32)

    def visit(state, item):
        best_now, chosen_now = state
        owner_index, cent_block, half_block = item
        scores = jnp.dot(embed_rows, cent_block.T, preferred_element_type=jnp.float32) - half_block[None, :]
        best_now = jnp.maximum(best_now, jnp.max(scores, axis=1))
        picked = (slot_ids[:, None] == column_ids) & (owner_ids[:, None] == owner_index)
        chosen_now = chosen_now + jnp.sum(jnp.where(picked, scores, jnp.zeros_like(scores)), axis=1)
        return (best_now, chosen_now), None

    start_state = (jnp.full((CROWS,), -jnp.inf, jnp.float32), jnp.zeros((CROWS,), jnp.float32))
    (best_all, chosen_all), _ = lax.scan(visit, start_state, (owner_range, cent_blocks, half_blocks))
    child_ids = owner_ids * K_DEV + slot_ids
    sums = jax.ops.segment_sum(embed_rows.astype(jnp.float32), child_ids, num_segments=CHILD)
    counts = jax.ops.segment_sum(jnp.ones((CROWS,), jnp.float32), child_ids, num_segments=CHILD)
    updated = (cent_rows.astype(jnp.float32) + sums) / (1.0 + counts)[:, None]
    return best_all - chosen_all, updated


def reference(embeddings, centroids, owner, slot):
    gap, new_centroids = lax.map(score_cluster, (embeddings, centroids, owner[:, :, 0], slot))
    return gap, new_centroids
```

```python
import functools
import jax
import jax.numpy as jnp
from jax import lax
from jax.experimental import pallas as pl
from jax.experimental.pallas import tpu as pltpu
from jax.sharding import PartitionSpec as P

MESH = pl.DeviceIdType.MESH
PARTS = 4
NT = (((1,), (1,)), ((), ()))


def kernel(
    n, emb, cent_hbm, owner_hbm, slot_hbm, gap_out, new_out,
    owner, slot, rows, cent, acc, ids, idrow, hn, rcp, res_out, res_in,
    recv, send_l, send_r, id_recv, id_send, res_recv, res_send, local,
):
    z = lax.axis_index("row")
    count = emb.shape[0]
    k_dev = cent.shape[0]
    rc = count // PARTS
    groups = n // PARTS

    def remote(src, dst, s_sem, r_sem, target):
        return pltpu.make_async_remote_copy(
            src_ref=src, dst_ref=dst, send_sem=s_sem, recv_sem=r_sem,
            device_id={"row": target}, device_id_type=MESH,
        )

    def place(b, c):
        return rows.at[pl.ds(pl.multiple_of((c * n + b) * rc, rc), rc)]

    def own_src(c):
        return emb.at[pl.ds(c * rc, rc)]

    def own_left(c):
        return remote(own_src(c), place(z, c), send_l.at[z, c], recv.at[z, c], z - 1)

    def own_right(c):
        return remote(own_src(c), place(z, c), send_r.at[z, c], recv.at[z, c], z + 1)

    def pass_left(b, c):
        return remote(place(b, c), place(b, c), send_l.at[b, c], recv.at[b, c], z - 1)

    def pass_right(b, c):
        return remote(place(b, c), place(b, c), send_r.at[b, c], recv.at[b, c], z + 1)

    def each_other(fn):
        if n <= 4:
            for o in range(1, n):
                fn(lax.rem(z + o, n))
        else:
            def step(o, carry):
                fn(lax.rem(z + o, n))
                return carry
            lax.fori_loop(1, n, step, 0)

    barrier = pltpu.get_barrier_semaphore()
    each_other(
        lambda t: pl.semaphore_signal(barrier, inc=1, device_id={"row": t}, device_id_type=MESH)
    )
    id_copies = [
        pltpu.make_async_copy(owner_hbm, owner, local.at[PARTS + 1]),
        pltpu.make_async_copy(slot_hbm, slot, local.at[PARTS + 2]),
    ]
    for copy in id_copies:
        copy.start()
    cent_copy = pltpu.make_async_copy(cent_hbm, cent, local.at[0])
    cent_copy.start()
    own_copies = [
        pltpu.make_async_copy(own_src(c), place(z, c), local.at[1 + c]) for c in range(PARTS)
    ]
    for copy in own_copies:
        copy.start()
    for copy in id_copies:
        copy.wait()
    ids[z] = owner[...] * k_dev + slot[...]
    pl.semaphore_wait(barrier, n - 1)

    for c in range(PARTS):
        @pl.when(z > 0)
        def _():
            own_left(c).start()

        @pl.when(z < n - 1)
        def _():
            own_right(c).start()

        if c == 0:
            each_other(
                lambda t: remote(ids.at[z], ids.at[z], id_send.at[t], id_recv.at[z], t).start()
            )

    cent_copy.wait()
    tile = min(128, k_dev)
    for k in range(0, k_dev, tile):
        block = cent[pl.ds(k, tile), :].astype(jnp.float32)
        hn[pl.ds(k, tile), :] = 0.5 * jnp.sum(block * block, axis=1, keepdims=True)
        acc[pl.ds(k, tile), :] = block
    for copy in own_copies:
        copy.wait()

    each_other(lambda t: remote(ids.at[z], ids.at[z], id_send.at[t], id_recv.at[t], t).wait_recv())
    lane_block = lax.broadcasted_iota(jnp.int32, (1, count), 1) // rc
    cent_ids = lax.broadcasted_iota(jnp.int32, (k_dev, count), 0)
    found = jnp.zeros((k_dev, count), jnp.float32)
    for g in range(groups):
        mine = [ids[g * PARTS + j] - z * k_dev for j in range(PARTS)]
        for c in range(PARTS):
            row = jnp.zeros((1, count), jnp.int32)
            for j in range(PARTS):
                shift = ((j - c) * rc) % count
                moved = mine[j] if shift == 0 else pltpu.roll(mine[j], shift, 1)
                row = jnp.where(lane_block == j, moved, row)
            idrow[g * PARTS + c] = row
            found = found + jnp.where(cent_ids == row, 1.0, 0.0)
    rcp[...] = 1.0 / (1.0 + jnp.sum(found, axis=1, keepdims=True))

    def gather_round(c):
        def step(s, carry):
            @pl.when(z + s < n)
            def _():
                pass_left(z + s, c).wait_recv()

                @pl.when(z > 0)
                def _():
                    pass_left(z + s, c).start()

            @pl.when(z - s >= 0)
            def _():
                pass_right(z - s, c).wait_recv()

                @pl.when(z < n - 1)
                def _():
                    pass_right(z - s, c).start()

            return carry

        lax.fori_loop(1, n, step, 0)

    def block_of(c, g):
        return rows[pl.ds(pl.multiple_of((c * n + g * PARTS) * rc, count), count), :]

    def over_groups(fn):
        if groups == 1:
            fn(0)
        else:
            def step(g, carry):
                fn(g)
                return carry
            lax.fori_loop(0, groups, step, 0)

    def score(c, g):
        scores = lax.dot_general(cent[...], block_of(c, g), NT, preferred_element_type=jnp.float32)
        scores = scores - hn[...]
        member = cent_ids == idrow[g * PARTS + c]
        res_out[g, pl.ds(c, 1), :] = jnp.max(scores, axis=0, keepdims=True)
        res_out[g, pl.ds(PARTS + c, 1), :] = jnp.sum(
            jnp.where(member, scores, 0.0), axis=0, keepdims=True
        )

    def sums(c, g, k):
        member = cent_ids[k:k + tile] == idrow[g * PARTS + c]
        return jnp.dot(
            jnp.where(member, 1.0, 0.0).astype(jnp.bfloat16), block_of(c, g),
            preferred_element_type=jnp.float32,
        )

    def add_sums(c, g):
        for k in range(0, k_dev, tile):
            acc[pl.ds(k, tile), :] += sums(c, g, k)

    for c in range(PARTS):
        gather_round(c)
        over_groups(functools.partial(score, c))
        if c < PARTS - 1:
            over_groups(functools.partial(add_sums, c))

    each_other(
        lambda t: remote(
            res_out.at[t // PARTS], res_in.at[z], res_send.at[t], res_recv.at[z], t
        ).start()
    )
    res_in[z] = res_out[z // PARTS]
    last = PARTS - 1
    if groups > 1:
        def step(g, carry):
            add_sums(last, g)
            return carry
        lax.fori_loop(0, groups - 1, step, 0)
    for k in range(0, k_dev, tile):
        total = acc[pl.ds(k, tile), :] + sums(last, groups - 1, k)
        new_out[pl.ds(k, tile), :] = total * rcp[pl.ds(k, tile), :]

    def wait_sends(c):
        def step(s, carry):
            @pl.when((z + s < n) & (z > 0))
            def _():
                pass_left(z + s, c).wait_send()

            @pl.when((z - s >= 0) & (z < n - 1))
            def _():
                pass_right(z - s, c).wait_send()

            return carry

        lax.fori_loop(0, n, step, 0)

    for c in range(PARTS):
        wait_sends(c)
    each_other(lambda t: remote(ids.at[z], ids.at[z], id_send.at[t], id_recv.at[t], t).wait_send())
    each_other(
        lambda t: remote(
            res_out.at[t // PARTS], res_in.at[t], res_send.at[t], res_recv.at[t], t
        ).wait()
    )
    got = res_in[...]
    best = jnp.max(got, axis=0)
    chosen = jnp.sum(got, axis=0)
    gap = best[0:PARTS] - chosen[PARTS:2 * PARTS]
    gap = pltpu.roll(gap, lax.rem((PARTS - lax.rem(z, PARTS)) * rc, count), 1)
    line = jnp.zeros((1, count), jnp.float32)
    for c in range(PARTS):
        moved = gap[c:c + 1] if c == 0 else pltpu.roll(gap[c:c + 1], c * rc, 1)
        line = jnp.where(lane_block == c, moved, line)
    gap_out[...] = line


def body(embeddings, centroids, owner, slot):
    n = lax.axis_size("row")
    count, width = embeddings.shape[1:]
    k_dev = centroids.shape[1]
    groups = n // PARTS
    vmem = pl.BlockSpec(memory_space=pltpu.VMEM)
    hbm = pl.BlockSpec(memory_space=pltpu.HBM)
    dma = pltpu.SemaphoreType.DMA
    gap, updated = pl.pallas_call(
        functools.partial(kernel, n),
        out_shape=(
            jax.ShapeDtypeStruct((1, count), jnp.float32),
            jax.ShapeDtypeStruct((k_dev, width), jnp.float32),
        ),
        in_specs=[hbm, hbm, hbm, hbm],
        out_specs=(vmem, vmem),
        scratch_shapes=[
            pltpu.VMEM((1, count), jnp.int32),
            pltpu.VMEM((1, count), jnp.int32),
            pltpu.VMEM((n * count, width), jnp.bfloat16),
            pltpu.VMEM((k_dev, width), jnp.bfloat16),
            pltpu.VMEM((k_dev, width), jnp.float32),
            pltpu.VMEM((n, 1, count), jnp.int32),
            pltpu.VMEM((n, 1, count), jnp.int32),
            pltpu.VMEM((k_dev, 1), jnp.float32),
            pltpu.VMEM((k_dev, 1), jnp.float32),
            pltpu.VMEM((groups, 2 * PARTS, count), jnp.float32),
            pltpu.VMEM((n, 2 * PARTS, count), jnp.float32),
            dma((n, PARTS)),
            dma((n, PARTS)),
            dma((n, PARTS)),
            dma((n,)),
            dma((n,)),
            dma((n,)),
            dma((n,)),
            dma((3 + PARTS,)),
        ],
        compiler_params=pltpu.CompilerParams(
            collective_id=0, has_side_effects=True, vmem_limit_bytes=40 * 2**20
        ),
    )(embeddings[0], centroids[0], owner[:, :, 0], slot)
    return gap, updated[None]


def solution(mesh):
    placed = (
        P(("group", "cent"), "row", None),
        P(("group", "cent"), "row", None),
        P(("group", "cent"), "row", None),
        P(("group", "cent"), "row"),
    )
    return jax.shard_map(
        body,
        mesh=mesh,
        in_specs=placed,
        out_specs=(P(("group", "cent"), "row"), P(("group", "cent"), "row", None)),
        check_vma=False,
    )
```

```python
import functools
import jax
import jax.numpy as jnp
from jax import lax
from jax.experimental import pallas as pl
from jax.experimental.pallas import tpu as pltpu
from jax.sharding import PartitionSpec as P

MESH = pl.DeviceIdType.MESH
PARTS = 4
NT = (((1,), (1,)), ((), ()))


def kernel(
    n, emb, cent_hbm, owner_hbm, slot_hbm, gap_out, new_out,
    owner, slot, rows, cent, ids, hn, rcp, res_out, res_in,
    recv, send_l, send_r, id_recv, id_send, res_recv, res_send, local,
):
    z = lax.axis_index("row")
    count = emb.shape[0]
    k_dev = cent.shape[0]
    rc = count // PARTS

    def remote(src, dst, s_sem, r_sem, target):
        return pltpu.make_async_remote_copy(
            src_ref=src, dst_ref=dst, send_sem=s_sem, recv_sem=r_sem,
            device_id={"row": target}, device_id_type=MESH,
        )

    def place(b, c):
        return rows.at[b, pl.ds(c * rc, rc)]

    def own_src(c):
        return emb.at[pl.ds(c * rc, rc)]

    def own_left(c):
        return remote(own_src(c), place(z, c), send_l.at[z, c], recv.at[z, c], z - 1)

    def own_right(c):
        return remote(own_src(c), place(z, c), send_r.at[z, c], recv.at[z, c], z + 1)

    def pass_left(b, c):
        return remote(place(b, c), place(b, c), send_l.at[b, c], recv.at[b, c], z - 1)

    def pass_right(b, c):
        return remote(place(b, c), place(b, c), send_r.at[b, c], recv.at[b, c], z + 1)

    def each_other(fn):
        if n <= 4:
            for o in range(1, n):
                fn(lax.rem(z + o, n))
        else:
            def step(o, carry):
                fn(lax.rem(z + o, n))
                return carry
            lax.fori_loop(1, n, step, 0)

    barrier = pltpu.get_barrier_semaphore()
    each_other(
        lambda t: pl.semaphore_signal(barrier, inc=1, device_id={"row": t}, device_id_type=MESH)
    )
    id_copies = [
        pltpu.make_async_copy(owner_hbm, owner, local.at[PARTS + 1]),
        pltpu.make_async_copy(slot_hbm, slot, local.at[PARTS + 2]),
    ]
    for copy in id_copies:
        copy.start()
    cent_copy = pltpu.make_async_copy(cent_hbm, cent, local.at[0])
    cent_copy.start()
    own_copies = [
        pltpu.make_async_copy(own_src(c), place(z, c), local.at[1 + c]) for c in range(PARTS)
    ]
    for copy in own_copies:
        copy.start()
    for copy in id_copies:
        copy.wait()
    ids[z] = owner[...] * k_dev + slot[...]
    pl.semaphore_wait(barrier, n - 1)

    for c in range(PARTS):
        @pl.when(z > 0)
        def _():
            own_left(c).start()

        @pl.when(z < n - 1)
        def _():
            own_right(c).start()

        if c == 0:
            each_other(
                lambda t: remote(ids.at[z], ids.at[z], id_send.at[t], id_recv.at[z], t).start()
            )

    cent_copy.wait()
    tile = min(128, k_dev)
    for k in range(0, k_dev, tile):
        block = cent[pl.ds(k, tile), :].astype(jnp.float32)
        hn[pl.ds(k, tile), :] = 0.5 * jnp.sum(block * block, axis=1, keepdims=True)
    for copy in own_copies:
        copy.wait()

    cent_ids = lax.broadcasted_iota(jnp.int32, (k_dev, count), 0)

    def member_of(b):
        return cent_ids == ids[b] - z * k_dev

    def score(b):
        scores = lax.dot_general(cent[...], rows[b], NT, preferred_element_type=jnp.float32)
        scores = scores - hn[...]
        best = jnp.max(scores, axis=0, keepdims=True)
        chosen = jnp.sum(jnp.where(member_of(b), scores, 0.0), axis=0, keepdims=True)
        return best, chosen

    def add_sums(b, first=False):
        member = jnp.where(member_of(b), 1.0, 0.0).astype(jnp.bfloat16)
        for k in range(0, k_dev, tile):
            part = jnp.dot(member[k:k + tile], rows[b], preferred_element_type=jnp.float32)
            here = pl.ds(k, tile)
            if first:
                new_out[here, :] = (cent[here, :].astype(jnp.float32) + part) * rcp[here, :]
            else:
                new_out[here, :] += part * rcp[here, :]

    def result(b):
        return remote(res_out.at[b], res_in.at[z], res_send.at[b], res_recv.at[z], b)

    def answer(b):
        best, chosen = score(b)
        res_out[b, 0:1, :] = best
        res_out[b, 1:2, :] = chosen
        result(b).start()

    each_other(lambda t: remote(ids.at[z], ids.at[z], id_send.at[t], id_recv.at[t], t).wait_recv())
    best, chosen = score(z)
    res_in[z, 0:1, :] = best
    res_in[z, 1:2, :] = chosen
    if n <= 4:
        found = sum(jnp.where(member_of(b), 1.0, 0.0) for b in range(n))
    else:
        found = lax.fori_loop(
            0, n, lambda b, f: f + jnp.where(member_of(b), 1.0, 0.0),
            jnp.zeros((k_dev, count), jnp.float32),
        )
    rcp[...] = 1.0 / (1.0 + jnp.sum(found, axis=1, keepdims=True))
    add_sums(z, True)

    def step(s, carry):
        for c in range(PARTS):
            @pl.when(z + s < n)
            def _():
                pass_left(z + s, c).wait_recv()

                @pl.when(z > 0)
                def _():
                    pass_left(z + s, c).start()

            @pl.when(z - s >= 0)
            def _():
                pass_right(z - s, c).wait_recv()

                @pl.when(z < n - 1)
                def _():
                    pass_right(z - s, c).start()

        @pl.when(z + s < n)
        def _():
            answer(z + s)

        @pl.when(z - s >= 0)
        def _():
            answer(z - s)

        @pl.when(z + s < n)
        def _():
            add_sums(z + s)

        @pl.when(z - s >= 0)
        def _():
            add_sums(z - s)

        return carry

    lax.fori_loop(1, n, step, 0)

    def wait_sends(s, carry):
        for c in range(PARTS):
            @pl.when((z + s < n) & (z > 0))
            def _():
                pass_left(z + s, c).wait_send()

            @pl.when((z - s >= 0) & (z < n - 1))
            def _():
                pass_right(z - s, c).wait_send()

        return carry

    lax.fori_loop(0, n, wait_sends, 0)
    each_other(lambda t: remote(ids.at[z], ids.at[z], id_send.at[t], id_recv.at[t], t).wait_send())
    each_other(
        lambda t: remote(res_out.at[t], res_in.at[t], res_send.at[t], res_recv.at[t], t).wait()
    )
    got = res_in[...]
    gap_out[...] = jnp.max(got[:, 0], axis=0, keepdims=True) - jnp.sum(got[:, 1], axis=0, keepdims=True)


def body(embeddings, centroids, owner, slot):
    n = lax.axis_size("row")
    count, width = embeddings.shape[1:]
    k_dev = centroids.shape[1]
    vmem = pl.BlockSpec(memory_space=pltpu.VMEM)
    hbm = pl.BlockSpec(memory_space=pltpu.HBM)
    dma = pltpu.SemaphoreType.DMA
    gap, updated = pl.pallas_call(
        functools.partial(kernel, n),
        out_shape=(
            jax.ShapeDtypeStruct((1, count), jnp.float32),
            jax.ShapeDtypeStruct((k_dev, width), jnp.float32),
        ),
        in_specs=[hbm, hbm, hbm, hbm],
        out_specs=(vmem, vmem),
        scratch_shapes=[
            pltpu.VMEM((1, count), jnp.int32),
            pltpu.VMEM((1, count), jnp.int32),
            pltpu.VMEM((n, count, width), jnp.bfloat16),
            pltpu.VMEM((k_dev, width), jnp.bfloat16),
            pltpu.VMEM((n, 1, count), jnp.int32),
            pltpu.VMEM((k_dev, 1), jnp.float32),
            pltpu.VMEM((k_dev, 1), jnp.float32),
            pltpu.VMEM((n, 2, count), jnp.float32),
            pltpu.VMEM((n, 2, count), jnp.float32),
            dma((n, PARTS)),
            dma((n, PARTS)),
            dma((n, PARTS)),
            dma((n,)),
            dma((n,)),
            dma((n,)),
            dma((n,)),
            dma((3 + PARTS,)),
        ],
        compiler_params=pltpu.CompilerParams(
            collective_id=0, has_side_effects=True, vmem_limit_bytes=56 * 2**20
        ),
    )(embeddings[0], centroids[0], owner[:, :, 0], slot)
    return gap, updated[None]


def solution(mesh):
    placed = (
        P(("group", "cent"), "row", None),
        P(("group", "cent"), "row", None),
        P(("group", "cent"), "row", None),
        P(("group", "cent"), "row"),
    )
    return jax.shard_map(
        body,
        mesh=mesh,
        in_specs=placed,
        out_specs=(P(("group", "cent"), "row"), P(("group", "cent"), "row", None)),
        check_vma=False,
    )
```

```python
import functools
import jax
import jax.numpy as jnp
from jax import lax
from jax.experimental import pallas as pl
from jax.experimental.pallas import tpu as pltpu
from jax.sharding import PartitionSpec as P

MESH = pl.DeviceIdType.MESH
PARTS = 4
NT = (((1,), (1,)), ((), ()))


def kernel(
    n, emb, cent_hbm, owner_hbm, slot_hbm, gap_out, rows_out, ids_out,
    owner, slot, rows, cent, ids, hn, res_out, res_in,
    recv, send_l, send_r, id_recv, id_send, res_recv, res_send, out_sem, local,
):
    z = lax.axis_index("row")
    count = emb.shape[0]
    k_dev = cent.shape[0]
    rc = count // PARTS

    def remote(src, dst, s_sem, r_sem, target):
        return pltpu.make_async_remote_copy(
            src_ref=src, dst_ref=dst, send_sem=s_sem, recv_sem=r_sem,
            device_id={"row": target}, device_id_type=MESH,
        )

    def place(b, c):
        return rows.at[b, pl.ds(c * rc, rc)]

    def own_src(c):
        return emb.at[pl.ds(c * rc, rc)]

    def own_left(c):
        return remote(own_src(c), place(z, c), send_l.at[z, c], recv.at[z, c], z - 1)

    def own_right(c):
        return remote(own_src(c), place(z, c), send_r.at[z, c], recv.at[z, c], z + 1)

    def pass_left(b, c):
        return remote(place(b, c), place(b, c), send_l.at[b, c], recv.at[b, c], z - 1)

    def pass_right(b, c):
        return remote(place(b, c), place(b, c), send_r.at[b, c], recv.at[b, c], z + 1)

    def each_other(fn):
        if n <= 4:
            for o in range(1, n):
                fn(lax.rem(z + o, n))
        else:
            def step(o, carry):
                fn(lax.rem(z + o, n))
                return carry
            lax.fori_loop(1, n, step, 0)

    barrier = pltpu.get_barrier_semaphore()
    each_other(
        lambda t: pl.semaphore_signal(barrier, inc=1, device_id={"row": t}, device_id_type=MESH)
    )
    id_copies = [
        pltpu.make_async_copy(owner_hbm, owner, local.at[PARTS + 1]),
        pltpu.make_async_copy(slot_hbm, slot, local.at[PARTS + 2]),
    ]
    for copy in id_copies:
        copy.start()
    cent_copy = pltpu.make_async_copy(cent_hbm, cent, local.at[0])
    cent_copy.start()
    own_copies = [
        pltpu.make_async_copy(own_src(c), place(z, c), local.at[1 + c]) for c in range(PARTS)
    ]
    for copy in own_copies:
        copy.start()
    for copy in id_copies:
        copy.wait()
    ids[z] = owner[...] * k_dev + slot[...]
    pl.semaphore_wait(barrier, n - 1)

    for c in range(PARTS):
        @pl.when(z > 0)
        def _():
            own_left(c).start()

        @pl.when(z < n - 1)
        def _():
            own_right(c).start()

        if c == 0:
            each_other(
                lambda t: remote(ids.at[z], ids.at[z], id_send.at[t], id_recv.at[z], t).start()
            )

    cent_copy.wait()
    tile = min(128, k_dev)
    for k in range(0, k_dev, tile):
        block = cent[pl.ds(k, tile), :].astype(jnp.float32)
        hn[pl.ds(k, tile), :] = 0.5 * jnp.sum(block * block, axis=1, keepdims=True)
    for copy in own_copies:
        copy.wait()

    cent_ids = lax.broadcasted_iota(jnp.int32, (k_dev, count), 0)

    def member_of(b):
        return cent_ids == ids[b] - z * k_dev

    def score(b):
        scores = lax.dot_general(cent[...], rows[b], NT, preferred_element_type=jnp.float32)
        scores = scores - hn[...]
        best = jnp.max(scores, axis=0, keepdims=True)
        chosen = jnp.sum(jnp.where(member_of(b), scores, 0.0), axis=0, keepdims=True)
        return best, chosen

    def keep(b):
        return pltpu.make_async_copy(rows.at[b], rows_out.at[b], out_sem.at[b])

    def result(b):
        return remote(res_out.at[b], res_in.at[z], res_send.at[b], res_recv.at[z], b)

    def answer(b):
        best, chosen = score(b)
        res_out[b, 0:1, :] = best
        res_out[b, 1:2, :] = chosen
        result(b).start()

    each_other(lambda t: remote(ids.at[z], ids.at[z], id_send.at[t], id_recv.at[t], t).wait_recv())
    best, chosen = score(z)
    res_in[z, 0:1, :] = best
    res_in[z, 1:2, :] = chosen
    keep(z).start()
    ids_out[...] = ids[...] - z * k_dev

    def step(s, carry):
        for c in range(PARTS):
            @pl.when(z + s < n)
            def _():
                pass_left(z + s, c).wait_recv()

                @pl.when(z > 0)
                def _():
                    pass_left(z + s, c).start()

            @pl.when(z - s >= 0)
            def _():
                pass_right(z - s, c).wait_recv()

                @pl.when(z < n - 1)
                def _():
                    pass_right(z - s, c).start()

        @pl.when(z + s < n)
        def _():
            keep(z + s).start()
            answer(z + s)

        @pl.when(z - s >= 0)
        def _():
            keep(z - s).start()
            answer(z - s)

        return carry

    lax.fori_loop(1, n, step, 0)

    def wait_sends(s, carry):
        for c in range(PARTS):
            @pl.when((z + s < n) & (z > 0))
            def _():
                pass_left(z + s, c).wait_send()

            @pl.when((z - s >= 0) & (z < n - 1))
            def _():
                pass_right(z - s, c).wait_send()

        return carry

    lax.fori_loop(0, n, wait_sends, 0)
    each_other(lambda t: remote(ids.at[z], ids.at[z], id_send.at[t], id_recv.at[t], t).wait_send())
    each_other(
        lambda t: remote(res_out.at[t], res_in.at[t], res_send.at[t], res_recv.at[t], t).wait()
    )
    lax.fori_loop(0, n, lambda b, carry: (keep(b).wait(), carry)[1], 0)
    got = res_in[...]
    gap_out[...] = jnp.max(got[:, 0], axis=0, keepdims=True) - jnp.sum(got[:, 1], axis=0, keepdims=True)


def finish(
    n, rows_hbm, cent_hbm, ids_hbm, gap_hbm, gap_out, new_hbm,
    rows, cent, ids, out, load, store, small,
):
    k_dev = cent.shape[0]
    count = ids.shape[-1]
    tile = min(128, k_dev)
    tiles = range(0, k_dev, tile)
    gap_copy = pltpu.make_async_copy(gap_hbm, gap_out, small.at[0])
    ids_copy = pltpu.make_async_copy(ids_hbm, ids, small.at[1])
    rows_copy = pltpu.make_async_copy(rows_hbm, rows, small.at[2])
    ids_copy.start()
    rows_copy.start()
    gap_copy.start()
    loads = [
        pltpu.make_async_copy(cent_hbm.at[pl.ds(k, tile)], cent.at[pl.ds(k, tile)], load.at[i])
        for i, k in enumerate(tiles)
    ]
    stores = [
        pltpu.make_async_copy(out.at[pl.ds(k, tile)], new_hbm.at[pl.ds(k, tile)], store.at[i])
        for i, k in enumerate(tiles)
    ]
    for copy in loads:
        copy.start()
    ids_copy.wait()
    lanes = lax.broadcasted_iota(jnp.int32, (tile, count), 0)

    def members(g, k):
        return jnp.concatenate(
            [
                jnp.where(lanes + k == ids[g * PARTS + j], 1.0, 0.0)
                for j in range(PARTS)
            ],
            axis=1,
        )

    def add(g, carry, k):
        total, found = carry
        member = members(g, k)
        block = rows[pl.ds(g * PARTS, PARTS)].reshape(PARTS * count, rows.shape[-1])
        total = total + jnp.dot(
            member.astype(jnp.bfloat16), block, preferred_element_type=jnp.float32
        )
        return total, found + jnp.sum(member, axis=1, keepdims=True)

    rows_copy.wait()
    for i, k in enumerate(tiles):
        loads[i].wait()
        here = pl.ds(k, tile)
        carry = (cent[here, :].astype(jnp.float32), jnp.ones((tile, 1), jnp.float32))
        if n == PARTS:
            total, found = add(0, carry, k)
        else:
            total, found = lax.fori_loop(0, n // PARTS, functools.partial(add, k=k), carry)
        out[here, :] = total * (1.0 / found)
        stores[i].start()
    for copy in stores:
        copy.wait()
    gap_copy.wait()


def body(embeddings, centroids, owner, slot):
    n = lax.axis_size("row")
    count, width = embeddings.shape[1:]
    k_dev = centroids.shape[1]
    tiles = k_dev // min(128, k_dev)
    vmem = pl.BlockSpec(memory_space=pltpu.VMEM)
    hbm = pl.BlockSpec(memory_space=pl.ANY)
    dma = pltpu.SemaphoreType.DMA
    gap, gathered, ids = pl.pallas_call(
        functools.partial(kernel, n),
        out_shape=(
            jax.ShapeDtypeStruct((1, count), jnp.float32),
            jax.ShapeDtypeStruct((n, count, width), jnp.bfloat16),
            jax.ShapeDtypeStruct((n, 1, count), jnp.int32),
        ),
        in_specs=[hbm, hbm, hbm, hbm],
        out_specs=(vmem, hbm, vmem),
        scratch_shapes=[
            pltpu.VMEM((1, count), jnp.int32),
            pltpu.VMEM((1, count), jnp.int32),
            pltpu.VMEM((n, count, width), jnp.bfloat16),
            pltpu.VMEM((k_dev, width), jnp.bfloat16),
            pltpu.VMEM((n, 1, count), jnp.int32),
            pltpu.VMEM((k_dev, 1), jnp.float32),
            pltpu.VMEM((n, 2, count), jnp.float32),
            pltpu.VMEM((n, 2, count), jnp.float32),
            dma((n, PARTS)),
            dma((n, PARTS)),
            dma((n, PARTS)),
            dma((n,)),
            dma((n,)),
            dma((n,)),
            dma((n,)),
            dma((n,)),
            dma((3 + PARTS,)),
        ],
        compiler_params=pltpu.CompilerParams(
            collective_id=0, has_side_effects=True, vmem_limit_bytes=56 * 2**20
        ),
    )(embeddings[0], centroids[0], owner[:, :, 0], slot)
    gap, updated = pl.pallas_call(
        functools.partial(finish, n),
        out_shape=(
            jax.ShapeDtypeStruct((1, count), jnp.float32),
            jax.ShapeDtypeStruct((k_dev, width), jnp.float32),
        ),
        in_specs=[hbm, hbm, hbm, hbm],
        out_specs=(hbm, hbm),
        scratch_shapes=[
            pltpu.VMEM((n, count, width), jnp.bfloat16),
            pltpu.VMEM((k_dev, width), jnp.bfloat16),
            pltpu.VMEM((n, 1, count), jnp.int32),
            pltpu.VMEM((k_dev, width), jnp.float32),
            dma((tiles,)),
            dma((tiles,)),
            dma((3,)),
        ],
        compiler_params=pltpu.CompilerParams(vmem_limit_bytes=56 * 2**20),
    )(gathered, centroids[0], ids, gap)
    return gap, updated[None]


def solution(mesh):
    placed = (
        P(("group", "cent"), "row", None),
        P(("group", "cent"), "row", None),
        P(("group", "cent"), "row", None),
        P(("group", "cent"), "row"),
    )
    return jax.shard_map(
        body,
        mesh=mesh,
        in_specs=placed,
        out_specs=(P(("group", "cent"), "row"), P(("group", "cent"), "row", None)),
        check_vma=False,
    )
```

```python
import functools
import jax
import jax.numpy as jnp
from jax import lax
from jax.experimental import pallas as pl
from jax.experimental.pallas import tpu as pltpu
from jax.sharding import PartitionSpec as P

MESH = pl.DeviceIdType.MESH
PARTS = 4
NT = (((1,), (1,)), ((), ()))


def kernel(
    n, emb, cent_hbm, owner_hbm, slot_hbm, gap_out, rows_out, ids_out,
    owner, slot, rows, cent, ids, hn, res_out, res_in,
    recv, send_l, send_r, id_recv, id_send, res_recv, res_send, out_sem, local,
):
    z = lax.axis_index("row")
    count = emb.shape[0]
    k_dev = cent.shape[0]
    rc = count // PARTS

    def remote(src, dst, s_sem, r_sem, target):
        return pltpu.make_async_remote_copy(
            src_ref=src, dst_ref=dst, send_sem=s_sem, recv_sem=r_sem,
            device_id={"row": target}, device_id_type=MESH,
        )

    def place(b, c):
        return rows.at[b, pl.ds(c * rc, rc)]

    def own_src(c):
        return emb.at[pl.ds(c * rc, rc)]

    def own_left(c):
        return remote(own_src(c), place(z, c), send_l.at[z, c], recv.at[z, c], z - 1)

    def own_right(c):
        return remote(own_src(c), place(z, c), send_r.at[z, c], recv.at[z, c], z + 1)

    def pass_left(b, c):
        return remote(place(b, c), place(b, c), send_l.at[b, c], recv.at[b, c], z - 1)

    def pass_right(b, c):
        return remote(place(b, c), place(b, c), send_r.at[b, c], recv.at[b, c], z + 1)

    def each_other(fn):
        if n <= 4:
            for o in range(1, n):
                fn(lax.rem(z + o, n))
        else:
            def step(o, carry):
                fn(lax.rem(z + o, n))
                return carry
            lax.fori_loop(1, n, step, 0)

    barrier = pltpu.get_barrier_semaphore()
    each_other(
        lambda t: pl.semaphore_signal(barrier, inc=1, device_id={"row": t}, device_id_type=MESH)
    )
    id_copies = [
        pltpu.make_async_copy(owner_hbm, owner, local.at[PARTS + 1]),
        pltpu.make_async_copy(slot_hbm, slot, local.at[PARTS + 2]),
    ]
    for copy in id_copies:
        copy.start()
    cent_copy = pltpu.make_async_copy(cent_hbm, cent, local.at[0])
    cent_copy.start()
    own_copies = [
        pltpu.make_async_copy(own_src(c), place(z, c), local.at[1 + c]) for c in range(PARTS)
    ]
    for copy in own_copies:
        copy.start()
    for copy in id_copies:
        copy.wait()
    ids[z] = owner[...] * k_dev + slot[...]
    pl.semaphore_wait(barrier, n - 1)

    for c in range(PARTS):
        @pl.when(z > 0)
        def _():
            own_left(c).start()

        @pl.when(z < n - 1)
        def _():
            own_right(c).start()

        if c == 0:
            each_other(
                lambda t: remote(ids.at[z], ids.at[z], id_send.at[t], id_recv.at[z], t).start()
            )

    cent_copy.wait()
    tile = min(128, k_dev)
    for k in range(0, k_dev, tile):
        block = cent[pl.ds(k, tile), :].astype(jnp.float32)
        hn[pl.ds(k, tile), :] = 0.5 * jnp.sum(block * block, axis=1, keepdims=True)
    for copy in own_copies:
        copy.wait()

    cent_ids = lax.broadcasted_iota(jnp.int32, (k_dev, count), 0)

    def member_of(b):
        return cent_ids == ids[b] - z * k_dev

    def score(b):
        scores = lax.dot_general(cent[...], rows[b], NT, preferred_element_type=jnp.float32)
        scores = scores - hn[...]
        best = jnp.max(scores, axis=0, keepdims=True)
        chosen = jnp.sum(jnp.where(member_of(b), scores, 0.0), axis=0, keepdims=True)
        return best, chosen

    def keep(b):
        return pltpu.make_async_copy(rows.at[b], rows_out.at[b], out_sem.at[b])

    def result(b):
        return remote(res_out.at[b], res_in.at[z], res_send.at[b], res_recv.at[z], b)

    def answer(b):
        best, chosen = score(b)
        res_out[b, 0:1, :] = best
        res_out[b, 1:2, :] = chosen
        result(b).start()

    each_other(lambda t: remote(ids.at[z], ids.at[z], id_send.at[t], id_recv.at[t], t).wait_recv())
    best, chosen = score(z)
    res_in[z, 0:1, :] = best
    res_in[z, 1:2, :] = chosen
    keep(z).start()
    ids_out[...] = ids[...] - z * k_dev

    def step(s, carry):
        for c in range(PARTS):
            @pl.when(z + s < n)
            def _():
                pass_left(z + s, c).wait_recv()

                @pl.when(z > 0)
                def _():
                    pass_left(z + s, c).start()

            @pl.when(z - s >= 0)
            def _():
                pass_right(z - s, c).wait_recv()

                @pl.when(z < n - 1)
                def _():
                    pass_right(z - s, c).start()

        @pl.when(z + s < n)
        def _():
            keep(z + s).start()
            answer(z + s)

        @pl.when(z - s >= 0)
        def _():
            keep(z - s).start()
            answer(z - s)

        return carry

    lax.fori_loop(1, n, step, 0)

    def wait_sends(s, carry):
        for c in range(PARTS):
            @pl.when((z + s < n) & (z > 0))
            def _():
                pass_left(z + s, c).wait_send()

            @pl.when((z - s >= 0) & (z < n - 1))
            def _():
                pass_right(z - s, c).wait_send()

        return carry

    lax.fori_loop(0, n, wait_sends, 0)
    each_other(lambda t: remote(ids.at[z], ids.at[z], id_send.at[t], id_recv.at[t], t).wait_send())
    each_other(
        lambda t: remote(res_out.at[t], res_in.at[t], res_send.at[t], res_recv.at[t], t).wait()
    )
    lax.fori_loop(0, n, lambda b, carry: (keep(b).wait(), carry)[1], 0)
    got = res_in[...]
    gap_out[...] = jnp.max(got[:, 0], axis=0, keepdims=True) - jnp.sum(got[:, 1], axis=0, keepdims=True)


def finish(
    n, rows_hbm, cent_hbm, ids_hbm, gap_hbm, gap_out, new_hbm,
    rows, cent, ids, out, member, load_rows, load_cent, store, small,
):
    tiles, k_dev, tile = cent.shape
    count = ids.shape[-1]
    gap_copy = pltpu.make_async_copy(gap_hbm, gap_out, small.at[0])
    ids_copy = pltpu.make_async_copy(ids_hbm, ids, small.at[1])
    ids_copy.start()
    loads, stores = [], []
    for i in range(tiles):
        columns = pl.ds(i * tile, tile)
        loads.append((
            pltpu.make_async_copy(rows_hbm.at[:, :, columns], rows.at[i], load_rows.at[i]),
            pltpu.make_async_copy(cent_hbm.at[:, columns], cent.at[i], load_cent.at[i]),
        ))
        stores.append(pltpu.make_async_copy(out.at[i], new_hbm.at[:, columns], store.at[i]))
        for copy in loads[i]:
            copy.start()
    gap_copy.start()
    ids_copy.wait()
    cent_ids = lax.broadcasted_iota(jnp.int32, (k_dev, count), 0)

    def mark(b, found):
        here = jnp.where(cent_ids == ids[b], 1.0, 0.0)
        lanes = b * count if n <= 4 else pl.multiple_of(b * count, count)
        member[:, pl.ds(lanes, count)] = here.astype(jnp.bfloat16)
        return found + here

    found = jnp.zeros((k_dev, count), jnp.float32)
    if n <= 4:
        for b in range(n):
            found = mark(b, found)
    else:
        found = lax.fori_loop(0, n, mark, found)
    rcp = 1.0 / (1.0 + jnp.sum(found, axis=1, keepdims=True))
    for i in range(tiles):
        for copy in loads[i]:
            copy.wait()
        total = cent[i].astype(jnp.float32) + jnp.dot(
            member[...], rows[i].reshape(n * count, tile), preferred_element_type=jnp.float32
        )
        out[i] = total * rcp
        stores[i].start()
    for copy in stores:
        copy.wait()
    gap_copy.wait()


def body(embeddings, centroids, owner, slot):
    n = lax.axis_size("row")
    count, width = embeddings.shape[1:]
    k_dev = centroids.shape[1]
    tile = min(256, width)
    tiles = width // tile
    vmem = pl.BlockSpec(memory_space=pltpu.VMEM)
    hbm = pl.BlockSpec(memory_space=pl.ANY)
    dma = pltpu.SemaphoreType.DMA
    gap, gathered, ids = pl.pallas_call(
        functools.partial(kernel, n),
        out_shape=(
            jax.ShapeDtypeStruct((1, count), jnp.float32),
            jax.ShapeDtypeStruct((n, count, width), jnp.bfloat16),
            jax.ShapeDtypeStruct((n, 1, count), jnp.int32),
        ),
        in_specs=[hbm, hbm, hbm, hbm],
        out_specs=(vmem, hbm, vmem),
        scratch_shapes=[
            pltpu.VMEM((1, count), jnp.int32),
            pltpu.VMEM((1, count), jnp.int32),
            pltpu.VMEM((n, count, width), jnp.bfloat16),
            pltpu.VMEM((k_dev, width), jnp.bfloat16),
            pltpu.VMEM((n, 1, count), jnp.int32),
            pltpu.VMEM((k_dev, 1), jnp.float32),
            pltpu.VMEM((n, 2, count), jnp.float32),
            pltpu.VMEM((n, 2, count), jnp.float32),
            dma((n, PARTS)),
            dma((n, PARTS)),
            dma((n, PARTS)),
            dma((n,)),
            dma((n,)),
            dma((n,)),
            dma((n,)),
            dma((n,)),
            dma((3 + PARTS,)),
        ],
        compiler_params=pltpu.CompilerParams(
            collective_id=0, has_side_effects=True, vmem_limit_bytes=56 * 2**20
        ),
    )(embeddings[0], centroids[0], owner[:, :, 0], slot)
    gap, updated = pl.pallas_call(
        functools.partial(finish, n),
        out_shape=(
            jax.ShapeDtypeStruct((1, count), jnp.float32),
            jax.ShapeDtypeStruct((k_dev, width), jnp.float32),
        ),
        in_specs=[hbm, hbm, hbm, hbm],
        out_specs=(hbm, hbm),
        scratch_shapes=[
            pltpu.VMEM((tiles, n, count, tile), jnp.bfloat16),
            pltpu.VMEM((tiles, k_dev, tile), jnp.bfloat16),
            pltpu.VMEM((n, 1, count), jnp.int32),
            pltpu.VMEM((tiles, k_dev, tile), jnp.float32),
            pltpu.VMEM((k_dev, n * count), jnp.bfloat16),
            dma((tiles,)),
            dma((tiles,)),
            dma((tiles,)),
            dma((2,)),
        ],
        compiler_params=pltpu.CompilerParams(vmem_limit_bytes=56 * 2**20),
    )(gathered, centroids[0], ids, gap)
    return gap, updated[None]


def solution(mesh):
    placed = (
        P(("group", "cent"), "row", None),
        P(("group", "cent"), "row", None),
        P(("group", "cent"), "row", None),
        P(("group", "cent"), "row"),
    )
    return jax.shard_map(
        body,
        mesh=mesh,
        in_specs=placed,
        out_specs=(P(("group", "cent"), "row"), P(("group", "cent"), "row", None)),
        check_vma=False,
    )
```

```python
import functools
import jax
import jax.numpy as jnp
from jax import lax
from jax.experimental import pallas as pl
from jax.experimental.pallas import tpu as pltpu
from jax.sharding import PartitionSpec as P

MESH = pl.DeviceIdType.MESH
PARTS = 4
NT = (((1,), (1,)), ((), ()))


def kernel(
    n, emb, cent_hbm, owner_hbm, slot_hbm, gap_out, rows_out, ids_out,
    owner, slot, rows, cent, ids, ids_near, hn, res_out, res_in,
    recv, send_l, send_r, id_recv, id_send, res_recv, res_send, out_sem, local,
):
    z = lax.axis_index("row")
    count = emb.shape[0]
    k_dev = cent.shape[0]
    rc = count // PARTS

    def remote(src, dst, s_sem, r_sem, target):
        return pltpu.make_async_remote_copy(
            src_ref=src, dst_ref=dst, send_sem=s_sem, recv_sem=r_sem,
            device_id={"row": target}, device_id_type=MESH,
        )

    def place(b, c):
        return rows.at[b, pl.ds(c * rc, rc)]

    def own_src(c):
        return emb.at[pl.ds(c * rc, rc)]

    def own_left(c):
        return remote(own_src(c), place(z, c), send_l.at[z, c], recv.at[z, c], z - 1)

    def own_right(c):
        return remote(own_src(c), place(z, c), send_r.at[z, c], recv.at[z, c], z + 1)

    def pass_left(b, c):
        return remote(place(b, c), place(b, c), send_l.at[b, c], recv.at[b, c], z - 1)

    def pass_right(b, c):
        return remote(place(b, c), place(b, c), send_r.at[b, c], recv.at[b, c], z + 1)

    def each_other(fn):
        if n <= 4:
            for o in range(1, n):
                fn(lax.rem(z + o, n))
        else:
            def step(o, carry):
                fn(lax.rem(z + o, n))
                return carry
            lax.fori_loop(1, n, step, 0)

    barrier = pltpu.get_barrier_semaphore()
    each_other(
        lambda t: pl.semaphore_signal(barrier, inc=1, device_id={"row": t}, device_id_type=MESH)
    )
    id_copies = [
        pltpu.make_async_copy(owner_hbm, owner, local.at[PARTS + 1]),
        pltpu.make_async_copy(slot_hbm, slot, local.at[PARTS + 2]),
    ]
    for copy in id_copies:
        copy.start()
    cent_copy = pltpu.make_async_copy(cent_hbm, cent, local.at[0])
    cent_copy.start()
    own_copies = [
        pltpu.make_async_copy(own_src(c), place(z, c), local.at[1 + c]) for c in range(PARTS)
    ]
    for copy in own_copies:
        copy.start()
    for copy in id_copies:
        copy.wait()
    ids[z] = owner[...] * k_dev + slot[...]
    pl.semaphore_wait(barrier, n - 1)

    for c in range(PARTS):
        @pl.when(z > 0)
        def _():
            own_left(c).start()

        @pl.when(z < n - 1)
        def _():
            own_right(c).start()

        if c == 0:
            each_other(
                lambda t: remote(ids.at[z], ids.at[z], id_send.at[t], id_recv.at[z], t).start()
            )

    cent_copy.wait()
    tile = min(128, k_dev)
    for k in range(0, k_dev, tile):
        block = cent[pl.ds(k, tile), :].astype(jnp.float32)
        hn[pl.ds(k, tile), :] = 0.5 * jnp.sum(block * block, axis=1, keepdims=True)
    for copy in own_copies:
        copy.wait()

    cent_ids = lax.broadcasted_iota(jnp.int32, (k_dev, count), 0)

    def member_of(b):
        return cent_ids == ids[b] - z * k_dev

    def score(b):
        scores = lax.dot_general(cent[...], rows[b], NT, preferred_element_type=jnp.float32)
        scores = scores - hn[...]
        best = jnp.max(scores, axis=0, keepdims=True)
        chosen = jnp.sum(jnp.where(member_of(b), scores, 0.0), axis=0, keepdims=True)
        return best, chosen

    def keep(b):
        return pltpu.make_async_copy(rows.at[b], rows_out.at[b], out_sem.at[b])

    def result(b):
        return remote(res_out.at[b], res_in.at[z], res_send.at[b], res_recv.at[z], b)

    def answer(b):
        best, chosen = score(b)
        res_out[b, 0:1, :] = best
        res_out[b, 1:2, :] = chosen
        result(b).start()

    each_other(lambda t: remote(ids.at[z], ids.at[z], id_send.at[t], id_recv.at[t], t).wait_recv())
    best, chosen = score(z)
    res_in[z, 0:1, :] = best
    res_in[z, 1:2, :] = chosen
    keep(z).start()
    ids_near[...] = ids[...] - z * k_dev
    ids_copy = pltpu.make_async_copy(ids_near, ids_out, out_sem.at[n])
    ids_copy.start()

    def step(s, carry):
        for c in range(PARTS):
            @pl.when(z + s < n)
            def _():
                pass_left(z + s, c).wait_recv()

                @pl.when(z > 0)
                def _():
                    pass_left(z + s, c).start()

            @pl.when(z - s >= 0)
            def _():
                pass_right(z - s, c).wait_recv()

                @pl.when(z < n - 1)
                def _():
                    pass_right(z - s, c).start()

        @pl.when(z + s < n)
        def _():
            keep(z + s).start()
            answer(z + s)

        @pl.when(z - s >= 0)
        def _():
            keep(z - s).start()
            answer(z - s)

        return carry

    lax.fori_loop(1, n, step, 0)

    def wait_sends(s, carry):
        for c in range(PARTS):
            @pl.when((z + s < n) & (z > 0))
            def _():
                pass_left(z + s, c).wait_send()

            @pl.when((z - s >= 0) & (z < n - 1))
            def _():
                pass_right(z - s, c).wait_send()

        return carry

    lax.fori_loop(0, n, wait_sends, 0)
    each_other(lambda t: remote(ids.at[z], ids.at[z], id_send.at[t], id_recv.at[t], t).wait_send())
    each_other(
        lambda t: remote(res_out.at[t], res_in.at[t], res_send.at[t], res_recv.at[t], t).wait()
    )
    lax.fori_loop(0, n, lambda b, carry: (keep(b).wait(), carry)[1], 0)
    ids_copy.wait()
    got = res_in[...]
    gap_out[...] = jnp.max(got[:, 0], axis=0, keepdims=True) - jnp.sum(got[:, 1], axis=0, keepdims=True)


def finish(
    n, rows_hbm, cent_hbm, ids_hbm, gap_hbm, gap_out, new_hbm,
    rows, cent, ids, out, member, load_rows, load, store, small,
):
    k_dev = cent.shape[0]
    count = ids.shape[-1]
    tile = min(128, k_dev)
    tiles = range(0, k_dev, tile)
    gap_copy = pltpu.make_async_copy(gap_hbm, gap_out, small.at[0])
    ids_copy = pltpu.make_async_copy(ids_hbm, ids, small.at[1])
    row_copies = [
        pltpu.make_async_copy(
            rows_hbm.at[pl.ds(p * n // PARTS, n // PARTS)],
            rows.at[pl.ds(p * n // PARTS, n // PARTS)],
            load_rows.at[p],
        )
        for p in range(PARTS)
    ]
    loads = [
        pltpu.make_async_copy(cent_hbm.at[pl.ds(k, tile)], cent.at[pl.ds(k, tile)], load.at[i])
        for i, k in enumerate(tiles)
    ]
    stores = [
        pltpu.make_async_copy(out.at[pl.ds(k, tile)], new_hbm.at[pl.ds(k, tile)], store.at[i])
        for i, k in enumerate(tiles)
    ]
    for copy in [ids_copy, *row_copies, *loads, gap_copy]:
        copy.start()
    ids_copy.wait()
    cent_ids = lax.broadcasted_iota(jnp.int32, (k_dev, count), 0)

    def mark(b, found):
        here = jnp.where(cent_ids == ids[b], 1.0, 0.0)
        lanes = b * count if n <= 4 else pl.multiple_of(b * count, count)
        member[:, pl.ds(lanes, count)] = here.astype(jnp.bfloat16)
        return found + here

    found = jnp.zeros((k_dev, count), jnp.float32)
    if n <= 4:
        for b in range(n):
            found = mark(b, found)
    else:
        found = lax.fori_loop(0, n, mark, found)
    rcp = 1.0 / (1.0 + jnp.sum(found, axis=1, keepdims=True))
    for copy in row_copies:
        copy.wait()

    def product(k, g):
        lanes = g * PARTS * count
        if n > PARTS:
            lanes = pl.multiple_of(lanes, count)
        block = rows[pl.ds(g * PARTS, PARTS)].reshape(PARTS * count, rows.shape[-1])
        return jnp.dot(
            member[pl.ds(k, tile), pl.ds(lanes, PARTS * count)], block,
            preferred_element_type=jnp.float32,
        )

    for i, k in enumerate(tiles):
        loads[i].wait()
        here = pl.ds(k, tile)
        total = cent[here, :].astype(jnp.float32)
        if n == PARTS:
            total = total + product(k, 0)
        else:
            total = lax.fori_loop(0, n // PARTS, lambda g, t: t + product(k, g), total)
        out[here, :] = total * rcp[k:k + tile]
        stores[i].start()
    for copy in stores:
        copy.wait()
    gap_copy.wait()


def body(embeddings, centroids, owner, slot):
    n = lax.axis_size("row")
    count, width = embeddings.shape[1:]
    k_dev = centroids.shape[1]
    tiles = k_dev // min(128, k_dev)
    vmem = pl.BlockSpec(memory_space=pltpu.VMEM)
    hbm = pl.BlockSpec(memory_space=pl.ANY)
    dma = pltpu.SemaphoreType.DMA
    gap, gathered, ids = pl.pallas_call(
        functools.partial(kernel, n),
        out_shape=(
            jax.ShapeDtypeStruct((1, count), jnp.float32),
            jax.ShapeDtypeStruct((n, count, width), jnp.bfloat16),
            jax.ShapeDtypeStruct((n, 1, count), jnp.int32),
        ),
        in_specs=[hbm, hbm, hbm, hbm],
        out_specs=(vmem, hbm, hbm),
        scratch_shapes=[
            pltpu.VMEM((1, count), jnp.int32),
            pltpu.VMEM((1, count), jnp.int32),
            pltpu.VMEM((n, count, width), jnp.bfloat16),
            pltpu.VMEM((k_dev, width), jnp.bfloat16),
            pltpu.VMEM((n, 1, count), jnp.int32),
            pltpu.VMEM((n, 1, count), jnp.int32),
            pltpu.VMEM((k_dev, 1), jnp.float32),
            pltpu.VMEM((n, 2, count), jnp.float32),
            pltpu.VMEM((n, 2, count), jnp.float32),
            dma((n, PARTS)),
            dma((n, PARTS)),
            dma((n, PARTS)),
            dma((n,)),
            dma((n,)),
            dma((n,)),
            dma((n,)),
            dma((n + 1,)),
            dma((3 + PARTS,)),
        ],
        compiler_params=pltpu.CompilerParams(
            collective_id=0, has_side_effects=True, vmem_limit_bytes=56 * 2**20
        ),
    )(embeddings[0], centroids[0], owner[:, :, 0], slot)
    gap, updated = pl.pallas_call(
        functools.partial(finish, n),
        out_shape=(
            jax.ShapeDtypeStruct((1, count), jnp.float32),
            jax.ShapeDtypeStruct((k_dev, width), jnp.float32),
        ),
        in_specs=[hbm, hbm, hbm, hbm],
        out_specs=(hbm, hbm),
        scratch_shapes=[
            pltpu.VMEM((n, count, width), jnp.bfloat16),
            pltpu.VMEM((k_dev, width), jnp.bfloat16),
            pltpu.VMEM((n, 1, count), jnp.int32),
            pltpu.VMEM((k_dev, width), jnp.float32),
            pltpu.VMEM((k_dev, n * count), jnp.bfloat16),
            dma((PARTS,)),
            dma((tiles,)),
            dma((tiles,)),
            dma((2,)),
        ],
        compiler_params=pltpu.CompilerParams(vmem_limit_bytes=56 * 2**20),
    )(gathered, centroids[0], ids, gap)
    return gap, updated[None]


def solution(mesh):
    placed = (
        P(("group", "cent"), "row", None),
        P(("group", "cent"), "row", None),
        P(("group", "cent"), "row", None),
        P(("group", "cent"), "row"),
    )
    return jax.shard_map(
        body,
        mesh=mesh,
        in_specs=placed,
        out_specs=(P(("group", "cent"), "row"), P(("group", "cent"), "row", None)),
        check_vma=False,
    )
```

```python
import functools
import jax
import jax.numpy as jnp
from jax import lax
from jax.experimental import pallas as pl
from jax.experimental.pallas import tpu as pltpu
from jax.sharding import PartitionSpec as P

MESH = pl.DeviceIdType.MESH
PARTS = 4
NT = (((1,), (1,)), ((), ()))


def kernel(
    n, emb, cent_hbm, owner_hbm, slot_hbm, gap_out, rows_out, ids_out,
    owner, slot, rows, cent, ids, hn, res_out, res_in,
    recv, send_l, send_r, id_recv, id_send, res_recv, res_send, out_sem, local,
):
    z = lax.axis_index("row")
    count = emb.shape[0]
    k_dev = cent.shape[0]
    rc = count // PARTS

    def remote(src, dst, s_sem, r_sem, target):
        return pltpu.make_async_remote_copy(
            src_ref=src, dst_ref=dst, send_sem=s_sem, recv_sem=r_sem,
            device_id={"row": target}, device_id_type=MESH,
        )

    def place(b, c):
        return rows.at[b, pl.ds(c * rc, rc)]

    def own_src(c):
        return emb.at[pl.ds(c * rc, rc)]

    def own_left(c):
        return remote(own_src(c), place(z, c), send_l.at[z, c], recv.at[z, c], z - 1)

    def own_right(c):
        return remote(own_src(c), place(z, c), send_r.at[z, c], recv.at[z, c], z + 1)

    def pass_left(b, c):
        return remote(place(b, c), place(b, c), send_l.at[b, c], recv.at[b, c], z - 1)

    def pass_right(b, c):
        return remote(place(b, c), place(b, c), send_r.at[b, c], recv.at[b, c], z + 1)

    def each_other(fn):
        if n <= 4:
            for o in range(1, n):
                fn(lax.rem(z + o, n))
        else:
            def step(o, carry):
                fn(lax.rem(z + o, n))
                return carry
            lax.fori_loop(1, n, step, 0)

    barrier = pltpu.get_barrier_semaphore()
    each_other(
        lambda t: pl.semaphore_signal(barrier, inc=1, device_id={"row": t}, device_id_type=MESH)
    )
    id_copies = [
        pltpu.make_async_copy(owner_hbm, owner, local.at[PARTS + 1]),
        pltpu.make_async_copy(slot_hbm, slot, local.at[PARTS + 2]),
    ]
    for copy in id_copies:
        copy.start()
    cent_copy = pltpu.make_async_copy(cent_hbm, cent, local.at[0])
    cent_copy.start()
    own_copies = [
        pltpu.make_async_copy(own_src(c), place(z, c), local.at[1 + c]) for c in range(PARTS)
    ]
    for copy in own_copies:
        copy.start()
    for copy in id_copies:
        copy.wait()
    ids[z] = owner[...] * k_dev + slot[...]
    pl.semaphore_wait(barrier, n - 1)

    for c in range(PARTS):
        @pl.when(z > 0)
        def _():
            own_left(c).start()

        @pl.when(z < n - 1)
        def _():
            own_right(c).start()

        if c == 0:
            each_other(
                lambda t: remote(ids.at[z], ids.at[z], id_send.at[t], id_recv.at[z], t).start()
            )

    cent_copy.wait()
    tile = min(128, k_dev)
    for k in range(0, k_dev, tile):
        block = cent[pl.ds(k, tile), :].astype(jnp.float32)
        hn[pl.ds(k, tile), :] = 0.5 * jnp.sum(block * block, axis=1, keepdims=True)
    for copy in own_copies:
        copy.wait()

    cent_ids = lax.broadcasted_iota(jnp.int32, (k_dev, count), 0)

    def member_of(b):
        return cent_ids == ids[b] - z * k_dev

    def score(b):
        scores = lax.dot_general(cent[...], rows[b], NT, preferred_element_type=jnp.float32)
        scores = scores - hn[...]
        best = jnp.max(scores, axis=0, keepdims=True)
        chosen = jnp.sum(jnp.where(member_of(b), scores, 0.0), axis=0, keepdims=True)
        return best, chosen

    def keep(b):
        return pltpu.make_async_copy(rows.at[b], rows_out.at[b], out_sem.at[b])

    def result(b):
        return remote(res_out.at[b], res_in.at[z], res_send.at[b], res_recv.at[z], b)

    def answer(b):
        best, chosen = score(b)
        res_out[b, 0:1, :] = best
        res_out[b, 1:2, :] = chosen
        result(b).start()

    each_other(lambda t: remote(ids.at[z], ids.at[z], id_send.at[t], id_recv.at[t], t).wait_recv())
    best, chosen = score(z)
    res_in[z, 0:1, :] = best
    res_in[z, 1:2, :] = chosen
    keep(z).start()
    ids_out[...] = ids[...] - z * k_dev

    def step(s, carry):
        for c in range(PARTS):
            @pl.when(z + s < n)
            def _():
                pass_left(z + s, c).wait_recv()

                @pl.when(z > 0)
                def _():
                    pass_left(z + s, c).start()

            @pl.when(z - s >= 0)
            def _():
                pass_right(z - s, c).wait_recv()

                @pl.when(z < n - 1)
                def _():
                    pass_right(z - s, c).start()

        @pl.when(z + s < n)
        def _():
            keep(z + s).start()
            answer(z + s)

        @pl.when(z - s >= 0)
        def _():
            keep(z - s).start()
            answer(z - s)

        return carry

    lax.fori_loop(1, n, step, 0)

    def wait_sends(s, carry):
        for c in range(PARTS):
            @pl.when((z + s < n) & (z > 0))
            def _():
                pass_left(z + s, c).wait_send()

            @pl.when((z - s >= 0) & (z < n - 1))
            def _():
                pass_right(z - s, c).wait_send()

        return carry

    lax.fori_loop(0, n, wait_sends, 0)
    each_other(lambda t: remote(ids.at[z], ids.at[z], id_send.at[t], id_recv.at[t], t).wait_send())
    each_other(
        lambda t: remote(res_out.at[t], res_in.at[t], res_send.at[t], res_recv.at[t], t).wait()
    )
    lax.fori_loop(0, n, lambda b, carry: (keep(b).wait(), carry)[1], 0)
    got = res_in[...]
    gap_out[...] = jnp.max(got[:, 0], axis=0, keepdims=True) - jnp.sum(got[:, 1], axis=0, keepdims=True)


def finish(
    n, rows_hbm, cent_hbm, ids_hbm, gap_hbm, gap_out, new_hbm,
    rows, cent, ids, out, counts, load, store, small,
):
    k_dev = cent.shape[0]
    count = ids.shape[-1]
    tile = min(256, k_dev)
    tiles = range(0, k_dev, tile)
    half = n // 2
    gap_copy = pltpu.make_async_copy(gap_hbm, gap_out, small.at[0])
    ids_copy = pltpu.make_async_copy(ids_hbm, ids, small.at[1])
    row_copies = [
        pltpu.make_async_copy(
            rows_hbm.at[pl.ds(p * half, half)], rows.at[pl.ds(p * half, half)], small.at[2 + p]
        )
        for p in range(2)
    ]
    loads = [
        pltpu.make_async_copy(cent_hbm.at[pl.ds(k, tile)], cent.at[pl.ds(k, tile)], load.at[i])
        for i, k in enumerate(tiles)
    ]
    stores = [
        pltpu.make_async_copy(out.at[pl.ds(k, tile)], new_hbm.at[pl.ds(k, tile)], store.at[i])
        for i, k in enumerate(tiles)
    ]
    for copy in [ids_copy, *row_copies, *loads, gap_copy]:
        copy.start()
    ids_copy.wait()
    lanes = lax.broadcasted_iota(jnp.int32, (tile, count), 0)

    def add(u, carry, k):
        total, found = carry
        member = jnp.concatenate(
            [jnp.where(lanes + k == ids[2 * u + j], 1.0, 0.0) for j in range(2)], axis=1
        )
        block = rows[pl.ds(2 * u, 2)].reshape(2 * count, rows.shape[-1])
        total = total + jnp.dot(
            member.astype(jnp.bfloat16), block, preferred_element_type=jnp.float32
        )
        return total, found + jnp.sum(member, axis=1, keepdims=True)

    def add_half(p, k, carry):
        units = half // 2
        if units == 1:
            return add(p, carry, k)
        return lax.fori_loop(p * units, (p + 1) * units, functools.partial(add, k=k), carry)

    row_copies[0].wait()
    for k in tiles:
        here = pl.ds(k, tile)
        zero = (jnp.zeros((tile, rows.shape[-1]), jnp.float32), jnp.ones((tile, 1), jnp.float32))
        out[here, :], counts[here, :] = add_half(0, k, zero)
    row_copies[1].wait()
    for i, k in enumerate(tiles):
        loads[i].wait()
        here = pl.ds(k, tile)
        carry = (out[here, :] + cent[here, :].astype(jnp.float32), counts[here, :])
        total, found = add_half(1, k, carry)
        out[here, :] = total * (1.0 / found)
        stores[i].start()
    for copy in stores:
        copy.wait()
    gap_copy.wait()


def body(embeddings, centroids, owner, slot):
    n = lax.axis_size("row")
    count, width = embeddings.shape[1:]
    k_dev = centroids.shape[1]
    tiles = k_dev // min(256, k_dev)
    vmem = pl.BlockSpec(memory_space=pltpu.VMEM)
    hbm = pl.BlockSpec(memory_space=pl.ANY)
    dma = pltpu.SemaphoreType.DMA
    gap, gathered, ids = pl.pallas_call(
        functools.partial(kernel, n),
        out_shape=(
            jax.ShapeDtypeStruct((1, count), jnp.float32),
            jax.ShapeDtypeStruct((n, count, width), jnp.bfloat16),
            jax.ShapeDtypeStruct((n, 1, count), jnp.int32),
        ),
        in_specs=[hbm, hbm, hbm, hbm],
        out_specs=(vmem, hbm, vmem),
        scratch_shapes=[
            pltpu.VMEM((1, count), jnp.int32),
            pltpu.VMEM((1, count), jnp.int32),
            pltpu.VMEM((n, count, width), jnp.bfloat16),
            pltpu.VMEM((k_dev, width), jnp.bfloat16),
            pltpu.VMEM((n, 1, count), jnp.int32),
            pltpu.VMEM((k_dev, 1), jnp.float32),
            pltpu.VMEM((n, 2, count), jnp.float32),
            pltpu.VMEM((n, 2, count), jnp.float32),
            dma((n, PARTS)),
            dma((n, PARTS)),
            dma((n, PARTS)),
            dma((n,)),
            dma((n,)),
            dma((n,)),
            dma((n,)),
            dma((n,)),
            dma((3 + PARTS,)),
        ],
        compiler_params=pltpu.CompilerParams(
            collective_id=0, has_side_effects=True, vmem_limit_bytes=56 * 2**20
        ),
    )(embeddings[0], centroids[0], owner[:, :, 0], slot)
    gap, updated = pl.pallas_call(
        functools.partial(finish, n),
        out_shape=(
            jax.ShapeDtypeStruct((1, count), jnp.float32),
            jax.ShapeDtypeStruct((k_dev, width), jnp.float32),
        ),
        in_specs=[hbm, hbm, hbm, hbm],
        out_specs=(hbm, hbm),
        scratch_shapes=[
            pltpu.VMEM((n, count, width), jnp.bfloat16),
            pltpu.VMEM((k_dev, width), jnp.bfloat16),
            pltpu.VMEM((n, 1, count), jnp.int32),
            pltpu.VMEM((k_dev, width), jnp.float32),
            pltpu.VMEM((k_dev, 1), jnp.float32),
            dma((tiles,)),
            dma((tiles,)),
            dma((4,)),
        ],
        compiler_params=pltpu.CompilerParams(vmem_limit_bytes=56 * 2**20),
    )(gathered, centroids[0], ids, gap)
    return gap, updated[None]


def solution(mesh):
    placed = (
        P(("group", "cent"), "row", None),
        P(("group", "cent"), "row", None),
        P(("group", "cent"), "row", None),
        P(("group", "cent"), "row"),
    )
    return jax.shard_map(
        body,
        mesh=mesh,
        in_specs=placed,
        out_specs=(P(("group", "cent"), "row"), P(("group", "cent"), "row", None)),
        check_vma=False,
    )
```
